32 devices in a mesh: dp: 8 (over y, x, core), tensor: 4 (over z).
Axes of the slice: x: 2, y: 2, z: 4, core: 2. Of those that a mesh axis runs over, the one named last changes fastest.
Arguments:
- activations: bfloat16 [3584, 8192], P('dp'), may hold values from -6 to 6
- grad_ragged: bfloat16 [3584, 14336], P('dp', 'tensor'), may hold values from -6 to 6
- master: float32 [8192, 7168], P('dp', 'tensor'), may hold values from -0.0625 to 0.0625
- momentum: float32 [8192, 7168], P('dp', 'tensor'), may hold values from -6 to 6
- offsets_full: int32 [8, 5], replicated, may hold values from 0 to 7168, as said below
- offsets_lost: int32 [4], replicated, may hold values from 0 to 7168, as said below
- failed: int32 [1], replicated, may hold values from 0 to 7
Outputs:
- input_grad: bfloat16 [3584, 8192], P('tensor', 'dp')
- new_momentum: float32 [8192, 7168], P('dp', 'tensor')
- new_master: float32 [8192, 7168], P('dp', 'tensor')
- new_weights: bfloat16 [8192, 7168], P(None, 'tensor')
The draws below stay inside these ranges and needn't reach their ends.
Inputs may be any that keep to these rules, and one draw needn't show every extreme that they name: `offsets_full`: each row holds 5 non-falling multiples of 128, the first 0 and the last 7168; no rank owns more than 28 blocks of 128 columns, and in every row some rank owns exactly 28. `offsets_lost`: 4 non-falling multiples of 128, the first 0 and the last 7168, bounds of the first 3 ranks; the last rank owns no column; no rank owns more than 28 blocks of 128 columns, and some rank owns exactly 28.
All inputs are finite; a program needn't handle non-finite values.
Results may differ from the reference program's by a relative error of at most 0.014.
Values may be sent and summed in bfloat16 or wider, within the bound.
A program may use at most 192 MiB of HBM per device.

```python
import math
import jax
import jax.numpy as jnp
from jax import lax

D = 8192
HID = 7168
TOK = 448
CAP = 3584
CANON = 1792
TOKENS = 3584
N_DP = 8
N_TENSOR = 4


def layout_bounds(key, rank_count, block_count, most_blocks):
    key_list = jax.random.split(key, 3)
    rank_ids = jnp.arange(rank_count, dtype=jnp.int32)
    shuffled = jax.random.permutation(key_list[0], rank_count).astype(jnp.int32)
    counts = block_count // rank_count + (shuffled < block_count % rank_count).astype(jnp.int32)
    top_rank = jax.random.randint(key_list[1], (), 0, rank_count).astype(jnp.int32)

    def lift(loop_step, loop_state):
        counts, sub_key = loop_state
        sub_key, pick_key = jax.random.split(sub_key)
        scores = jax.random.randint(pick_key, (rank_count,), 0, 1 << 20) * rank_count + rank_ids
        eligible = (counts > 0) & (rank_ids != top_rank)
        donor_rank = jnp.argmax(jnp.where(eligible, scores, -1))
        needs_more = counts[top_rank] < most_blocks
        moved = (rank_ids == top_rank).astype(jnp.int32) - (rank_ids == donor_rank).astype(jnp.int32)
        return (counts + jnp.where(needs_more, moved, 0), sub_key)
    counts, sub_key = lax.fori_loop(0, most_blocks, lift, (counts, key_list[2]))

    def wander(loop_step, loop_state):
        counts, sub_key = loop_state
        sub_key, pick_give, pick_take = jax.random.split(sub_key, 3)
        give_scores = jax.random.randint(pick_give, (rank_count,), 0, 1 << 20) * rank_count + rank_ids
        take_scores = jax.random.randint(pick_take, (rank_count,), 0, 1 << 20) * rank_count + rank_ids
        can_give = (counts > 0) & (rank_ids != top_rank)
        can_take = (counts < most_blocks) & (rank_ids != top_rank)
        giver_rank = jnp.argmax(jnp.where(can_give, give_scores, -1))
        taker_rank = jnp.argmax(jnp.where(can_take, take_scores, -1))
        movable = jnp.any(can_give) & jnp.any(can_take) & (giver_rank != taker_rank)
        moved = (rank_ids == taker_rank).astype(jnp.int32) - (rank_ids == giver_rank).astype(jnp.int32)
        return (counts + jnp.where(movable, moved, 0), sub_key)
    counts, _ = lax.fori_loop(0, 16 * rank_count, wander, (counts, sub_key))
    return jnp.concatenate([jnp.zeros((1,), jnp.int32), jnp.cumsum(counts).astype(jnp.int32) * 128])


def draw_offsets_full(key, part):
    most_blocks = 2 * HID // (128 * N_TENSOR)
    replica_keys = jax.random.split(jax.random.fold_in(key, 11), N_DP)
    rows = jax.vmap(lambda one_key: layout_bounds(one_key, N_TENSOR, HID // 128, most_blocks))(replica_keys)
    pick_first = jax.random.randint(jax.random.fold_in(key, 31), (), 0, N_DP).astype(jnp.int32)
    pick_step = jax.random.randint(jax.random.fold_in(key, 37), (), 1, N_DP).astype(jnp.int32)
    pick_second = (pick_first + pick_step) % N_DP
    rank_ids = jnp.arange(N_TENSOR, dtype=jnp.int32)
    skew_counts = jnp.where(rank_ids < N_TENSOR // 2, 0, most_blocks).astype(jnp.int32)
    skew_row = jnp.concatenate([jnp.zeros((1,), jnp.int32), jnp.cumsum(skew_counts).astype(jnp.int32) * 128])
    row_ids = jnp.arange(N_DP, dtype=jnp.int32)
    chosen = (row_ids == pick_first) | (row_ids == pick_second)
    return jnp.where(chosen[:, None], skew_row[None, :], rows).astype(jnp.int32)


def draw_offsets_lost(key, part):
    most_blocks = 2 * HID // (128 * N_TENSOR)
    return layout_bounds(jax.random.fold_in(key, 23), N_TENSOR - 1, HID // 128, most_blocks)


def level_of(stream_key, dims, cuts, least, high):
    loudness, own = 1.0, jax.random.fold_in(stream_key, 6)
    for dim, shards_of in cuts:
        draws = jnp.exp(jax.random.uniform(jax.random.fold_in(own, dim), (shards_of,), jnp.float32, least / len(cuts), high / len(cuts)))
        loudness = loudness * jnp.repeat(draws, dims[dim] // shards_of).reshape([-1 if axis == dim else 1 for axis in range(len(dims))])
    return loudness


def bell_draw(rng, extent, spread, limit, shards=(), kind=jnp.bfloat16):
    drawn = jax.random.normal(rng, extent, jnp.float32) * spread
    if len(shards) > 0:
        drawn = level_of(rng, extent, shards, -0.22, 0.18) * drawn
    return jnp.clip(drawn, min=-limit, max=limit).astype(kind)


def setup_inputs(seed: int = 0) -> dict:
    keys = jax.random.split(jax.random.key(seed), 8)
    activations = bell_draw(keys[0], (TOKENS, D), 1.0, 6.0, ((0, 8),))
    grad_ragged = bell_draw(keys[1], (TOKENS, N_TENSOR * CAP), 1.0, 6.0, ((0, 8), (1, 4)))
    master = bell_draw(keys[2], (D, HID), D ** -0.5, 0.0625, ((0, 8), (1, 4)), jnp.float32)
    momentum = bell_draw(keys[3], (D, HID), 1.0, 6.0, ((0, 8), (1, 4)), jnp.float32)
    offsets_full = draw_offsets_full(jax.random.fold_in(keys[7], 71), 0)
    offsets_lost = draw_offsets_lost(jax.random.fold_in(keys[7], 71), 0)
    failed = jax.random.randint(keys[6], (1,), 0, N_DP).astype(jnp.int32)
    return dict(activations=activations, grad_ragged=grad_ragged, master=master, momentum=momentum, offsets_full=offsets_full, offsets_lost=offsets_lost, failed=failed)


def bounds_of(replica, offsets_full, offsets_lost, failed):
    lost_row = jnp.concatenate([offsets_lost, jnp.full((1,), HID, jnp.int32)])
    return jnp.where(failed[0] == replica, lost_row, offsets_full[replica])

def reference(activations, grad_ragged, master, momentum, offsets_full, offsets_lost, failed):
    columns = jnp.arange(HID, dtype=jnp.int32)
    grad_scale = 1.0 / math.sqrt(TOKENS)

    def densify(replica):
        bounds = bounds_of(replica, offsets_full, offsets_lost, failed)
        owner_rank = lax.optimization_barrier(jnp.sum((bounds[None, 1:N_TENSOR] <= columns[:, None]).astype(jnp.int32), axis=1))
        col_index = (owner_rank * CAP + columns - bounds[owner_rank]).astype(jnp.int32)
        rep_rows = lax.dynamic_slice_in_dim(grad_ragged, replica * TOK, TOK, 0)
        return jnp.take(rep_rows, col_index, axis=1)
    dense_grads = lax.map(densify, jnp.arange(N_DP, dtype=jnp.int32))

    def accumulate(running, replica):
        act_rows = lax.dynamic_slice_in_dim(activations, replica * TOK, TOK, 0)
        partial_value = jnp.dot(act_rows.T, dense_grads[replica], preferred_element_type=jnp.float32) * grad_scale
        rounded = lax.optimization_barrier(partial_value.astype(jnp.bfloat16))
        return (running + rounded.astype(jnp.float32), None)
    weight_grad, _ = lax.scan(accumulate, jnp.zeros((D, HID), jnp.float32), jnp.arange(N_DP, dtype=jnp.int32))
    new_momentum = 0.9 * momentum + weight_grad
    new_master = master - 0.01 * new_momentum
    new_weights = new_master.astype(jnp.bfloat16)
    working = master.astype(jnp.bfloat16)
    flat_grads = dense_grads.reshape(TOKENS, HID)

    def add_block(running, col_block):
        grad_cols = lax.dynamic_slice_in_dim(flat_grads, col_block * CANON, CANON, 1)
        weight_cols = lax.dynamic_slice_in_dim(working, col_block * CANON, CANON, 1)
        partial_value = jnp.dot(grad_cols, weight_cols.T, preferred_element_type=jnp.float32)
        rounded = lax.optimization_barrier(partial_value.astype(jnp.bfloat16))
        return (running + rounded.astype(jnp.float32), None)
    input_sum, _ = lax.scan(add_block, jnp.zeros((TOKENS, D), jnp.float32), jnp.arange(N_TENSOR, dtype=jnp.int32))
    return (input_sum.astype(jnp.bfloat16), new_momentum, new_master, new_weights)
```

```python
import math

import jax
import jax.numpy as jnp
from jax import lax
from jax.experimental import pallas as pl
from jax.experimental.pallas import tpu as pltpu
from jax.sharding import PartitionSpec as P

LANE = 128
VMEM_BYTES = 56 * 1024 * 1024
F32, BF16 = jnp.float32, jnp.bfloat16


def reach(ranks, width, canonical):
    hidden = canonical * ranks
    spans = []
    for t in range(ranks):
        lo, hi = max(0, hidden - width * (ranks - t)), min(hidden, width * (t + 1))
        spans.append(range(lo // canonical, -(-hi // canonical)))
    return spans


def place_kernel(offsets, canonical, info, buf, out):
    first, owned, rank = info[0], info[1], info[2]
    per_block = canonical // LANE
    for k, offset in enumerate(offsets):

        def body(j, carry):
            src = (rank + offset) * per_block + j - first
            valid = (src >= 0) & (src < owned)
            dst = pl.ds(pl.multiple_of(j * LANE, LANE), LANE)

            @pl.when(valid)
            def _():
                out[k, :, dst] = buf[:, pl.ds(pl.multiple_of(src * LANE, LANE), LANE)]

            @pl.when(jnp.logical_not(valid))
            def _():
                out[k, :, dst] = jnp.zeros((buf.shape[0], LANE), buf.dtype)

            return carry

        lax.fori_loop(0, per_block, body, 0)


def place(buf, info, offsets, canonical):
    rows = buf.shape[0]
    return pl.pallas_call(
        lambda *refs: place_kernel(offsets, canonical, *refs),
        out_shape=jax.ShapeDtypeStruct((len(offsets), rows, canonical), BF16),
        in_specs=[pl.BlockSpec(memory_space=pltpu.SMEM), pl.BlockSpec(memory_space=pltpu.VMEM)],
        out_specs=pl.BlockSpec(memory_space=pltpu.VMEM),
        compiler_params=pltpu.CompilerParams(vmem_limit_bytes=VMEM_BYTES),
        name="place",
    )(info, buf)


def update_kernel(scale, feats, grads, master, momentum, new_mom, new_mas, new_w, total):
    replicas, _, width = grads.shape
    rows = feats.shape[2]
    total[...] = jnp.zeros_like(total)

    def body(r, carry):
        lhs = feats[r].T
        for lo in range(0, width, 256):
            hi = min(lo + 256, width)
            part = jnp.dot(lhs, grads[r, :, lo:hi], preferred_element_type=F32) * scale
            total[:, lo:hi] += part.astype(BF16).astype(F32)
        return carry

    lax.fori_loop(0, replicas, body, 0)
    mom = 0.9 * momentum[...] + total[...]
    mas = master[...] - 0.01 * mom
    new_mom[...] = mom
    new_mas[...] = mas
    new_w[...] = mas.astype(BF16)


def update(feats, grads, master, momentum, scale):
    replicas, toks, own = feats.shape
    width = master.shape[1]
    rows = math.gcd(own, 256)
    tile = pl.BlockSpec((rows, width), lambda i: (i, 0))
    return pl.pallas_call(
        lambda *refs: update_kernel(scale, *refs),
        grid=(own // rows,),
        out_shape=(
            jax.ShapeDtypeStruct(master.shape, F32),
            jax.ShapeDtypeStruct(master.shape, F32),
            jax.ShapeDtypeStruct(master.shape, BF16),
        ),
        in_specs=[
            pl.BlockSpec((replicas, toks, rows), lambda i: (0, 0, i)),
            pl.BlockSpec(grads.shape, lambda i: (0, 0, 0), pipeline_mode=pl.Buffered(1)),
            tile,
            tile,
        ],
        out_specs=(tile, tile, tile),
        scratch_shapes=[pltpu.VMEM((rows, width), F32)],
        compiler_params=pltpu.CompilerParams(vmem_limit_bytes=VMEM_BYTES),
        cost_estimate=pl.CostEstimate(
            flops=2 * replicas * toks * own * width, bytes_accessed=60 * 2**20, transcendentals=0
        ),
        name="update",
    )(feats, grads, master, momentum)


def inputs_kernel(grads, master, out):
    weights = master[...].astype(BF16)

    def body(r, carry):
        out[r] = lax.dot_general(
            grads[r], weights, (((1,), (1,)), ((), ())), preferred_element_type=F32
        ).astype(BF16)
        return carry

    lax.fori_loop(0, grads.shape[0], body, 0)


def inputs(grads, master):
    replicas, toks, width = grads.shape
    own = master.shape[0]
    rows = math.gcd(own, 256)
    return pl.pallas_call(
        inputs_kernel,
        grid=(own // rows,),
        out_shape=jax.ShapeDtypeStruct((replicas, toks, own), BF16),
        in_specs=[
            pl.BlockSpec(grads.shape, lambda i: (0, 0, 0), pipeline_mode=pl.Buffered(1)),
            pl.BlockSpec((rows, width), lambda i: (i, 0)),
        ],
        out_specs=pl.BlockSpec((replicas, toks, rows), lambda i: (0, 0, i)),
        compiler_params=pltpu.CompilerParams(vmem_limit_bytes=VMEM_BYTES),
        cost_estimate=pl.CostEstimate(
            flops=2 * replicas * toks * own * width, bytes_accessed=30 * 2**20, transcendentals=0
        ),
        name="inputs",
    )(grads, master)


def line_scatter(part, axis, ranks):
    rank = lax.axis_index(axis)
    rows = part.shape[0] // ranks

    def chunk(q):
        return lax.dynamic_slice_in_dim(part, jnp.clip(q, 0, ranks - 1) * rows, rows, 0)

    right = left = None
    for step in range(ranks - 1):
        to_right = chunk(ranks - 1 - step + rank)
        to_left = chunk(step - (ranks - 1 - rank))
        if right is not None:
            to_right = (to_right.astype(F32) + right.astype(F32)).astype(BF16)
            to_left = (to_left.astype(F32) + left.astype(F32)).astype(BF16)
        right = lax.ppermute(to_right, axis, [(t, t + 1) for t in range(step + 1)])
        left = lax.ppermute(
            to_left, axis, [(ranks - 1 - t, ranks - 2 - t) for t in range(step + 1)]
        )
    mine = chunk(rank).astype(F32)
    return (mine + right.astype(F32) + left.astype(F32)).astype(BF16)


def local(activations, grad_ragged, master, momentum, offsets_full, offsets_lost, failed):
    replicas = lax.axis_size("dp")
    ranks = lax.axis_size("tensor")
    replica = lax.axis_index("dp")
    rank = lax.axis_index("tensor")
    toks = activations.shape[0]
    own, canonical = master.shape
    hidden = canonical * ranks
    scale = 1.0 / math.sqrt(toks * replicas)

    feats = activations.reshape(toks, replicas, own).transpose(1, 0, 2)
    feats = lax.all_to_all(feats, "dp", split_axis=0, concat_axis=0, tiled=True)

    lost_row = jnp.concatenate([offsets_lost, jnp.full((1,), hidden, jnp.int32)])
    full_row = lax.dynamic_index_in_dim(offsets_full, replica, 0, keepdims=False)
    bounds = jnp.where(failed[0] == replica, lost_row, full_row) // LANE
    first = lax.dynamic_index_in_dim(bounds, rank, 0, keepdims=False)
    last = lax.dynamic_index_in_dim(bounds, rank + 1, 0, keepdims=False)
    info = jnp.stack([first, last - first, rank]).astype(jnp.int32)

    spans = reach(ranks, grad_ragged.shape[1], canonical)
    pairs = {}
    for t, span in enumerate(spans):
        for q in span:
            pairs.setdefault(q - t, []).append((t, q))
    offsets = [0] + sorted((d for d in pairs if d), key=lambda d: (-abs(d), d))
    placed = place(grad_ragged, info, offsets, canonical)
    home = placed[0]
    for k, d in enumerate(offsets[1:]):
        home = home + lax.ppermute(placed[k + 1], "tensor", pairs[d])

    grads = lax.all_gather(home, "dp", axis=0)
    new_momentum, new_master, shard = update(feats, grads, master, momentum, scale)
    new_weights = lax.all_gather(shard, "dp", axis=0, tiled=True)
    part = inputs(grads, master)
    input_grad = line_scatter(part.reshape(replicas * toks, own), "tensor", ranks)
    return (input_grad, new_momentum, new_master, new_weights)


def solution(mesh):
    placed = (P("dp", None), P("dp", "tensor"), P("dp", "tensor"), P("dp", "tensor"), P(), P(), P())
    return jax.shard_map(
        local,
        mesh=mesh,
        in_specs=placed,
        out_specs=(P("tensor", "dp"), P("dp", "tensor"), P("dp", "tensor"), P(None, "tensor")),
        check_vma=False,
    )
```
